32 devices in a mesh: dp: 8 (over y, x, core), tensor: 4 (over z).
Axes of the slice: x: 2, y: 2, z: 4, core: 2. Of those that a mesh axis runs over, the one named last changes fastest.
Arguments:
- gate_pre: bfloat16 [4096, 14336], P('dp', 'tensor'), may hold values from -6 to 6
- up_pre: bfloat16 [4096, 14336], P('dp', 'tensor'), may hold values from -6 to 6
- grad_out: bfloat16 [4096, 4096], P(('dp', 'tensor')), may hold values from -6 to 6
- codes: bfloat16 [14336, 4096], P('tensor'), as said below
- scales: int32 [448, 4096], P('tensor'), may hold values from 117 to 120
Outputs:
- out: bfloat16 [4096, 4096], P(('dp', 'tensor'))
- grad_gate: bfloat16 [4096, 14336], P('dp', 'tensor')
- grad_up: bfloat16 [4096, 14336], P('dp', 'tensor')
- grad_weight: bfloat16 [14336, 4096], P('tensor', 'dp')
The draws below stay inside these ranges and needn't reach their ends.
Inputs may be any that keep to these rules, and one draw needn't show every extreme that they name: `codes`: every entry is an FP8 E4M3 normal value (sign, exponent field 4 to 9, three mantissa bits), held exactly.
All inputs are finite; a program needn't handle non-finite values.
Results may differ from the reference program's by a relative error of at most 0.022.
Values may be sent and summed in bfloat16 or wider, within the bound.
A program may use at most 192 MiB of HBM per device.

```python
import jax
import jax.numpy as jnp
from jax import lax

D = 4096
FF = 14336
TOK_DEV = 512
TOKENS = 4096
N_DP = 8
N_TENSOR = 4


def draw_codes(key, part):
    key_sign, key_expo, key_mant = jax.random.split(key, 3)
    sign_bits = jax.random.randint(key_sign, (FF, D), 0, 2)
    exponent = jax.random.randint(key_expo, (FF, D), 4, 10)
    mantissa = jax.random.randint(key_mant, (FF, D), 0, 8)
    value = (1.0 - 2.0 * sign_bits.astype(jnp.float32)) * (1.0 + mantissa.astype(jnp.float32) / 8.0) * jnp.exp2(exponent.astype(jnp.float32) - 7.0)
    return value.astype(jnp.bfloat16)


def with_ends(entries, key, smallest, high):
    place = [jax.random.randint(jax.random.fold_in(key, axis), (), 0, length) for axis, length in enumerate(entries.shape)]
    longest = entries.shape.index(max(entries.shape))
    next_to = place[:longest] + [(place[longest] + 1) % entries.shape[longest]] + place[longest + 1:]
    return entries.at[tuple(place)].set(smallest).at[tuple(next_to)].set(high)


def strengthened(values, stream_key, source, target, blocks, factor):
    owner, partner = [(jnp.arange(values.shape[dim]) // (values.shape[dim] // blocks)).reshape([-1 if axis == dim else 1 for axis in range(values.ndim)]) for dim in (source, target)]
    chosen = jax.random.permutation(stream_key, blocks)[partner]
    strong = (owner == chosen) | (owner == (partner + blocks // 2) % blocks)
    return jnp.where(strong, factor * values, values)


def block_scale(rng, extent, shards, least, largest):
    gain, own = 1.0, jax.random.fold_in(rng, 6)
    for dim, blocks in shards:
        heights = jnp.exp(jax.random.uniform(jax.random.fold_in(own, dim), (blocks,), jnp.float32, least / len(shards), largest / len(shards)))
        gain = gain * jnp.repeat(heights, extent[dim] // blocks).reshape([-1 if axis == dim else 1 for axis in range(len(extent))])
    return gain


def bell_draw(rng, extent, deviation, limit, pieces=(), kind=jnp.bfloat16):
    factor_of = block_scale(rng, extent, pieces, -0.22, 0.18) if pieces else 1.0
    drawn = jax.random.normal(rng, extent, jnp.float32) * deviation * factor_of
    return jnp.minimum(jnp.maximum(drawn, -limit), limit).astype(kind)


def gaussian_with(own_key, extent, deviation, bound, cuts, heavy, held_as=jnp.bfloat16):
    entries = deviation * jax.random.normal(own_key, extent, jnp.float32)
    if cuts:
        entries = entries * block_scale(own_key, extent, cuts, -0.22, 0.18)
    return jnp.clip(strengthened(entries, jax.random.fold_in(own_key, 3), *heavy), -bound, bound).astype(held_as)


def setup_inputs(seed: int = 0) -> dict:
    arg_keys = jax.random.split(jax.random.key(seed), 6)
    gate_pre = bell_draw(arg_keys[0], (TOKENS, FF), 1.0, 6.0, ((0, 8), (1, 4)))
    up_pre = bell_draw(arg_keys[1], (TOKENS, FF), 1.0, 6.0, ((0, 8), (1, 4)))
    grad_out = gaussian_with(arg_keys[2], (TOKENS, D), 1.0, 6.0, ((0, 32),), (0, 1, 32, 2.75))
    codes = draw_codes(jax.random.fold_in(arg_keys[5], 71), 0)
    scales = with_ends(jax.random.randint(arg_keys[4], (FF // 32, D), 117, 121), jax.random.fold_in(arg_keys[4], 1), 117, 120).astype(jnp.int32)
    return {"gate_pre": gate_pre, "up_pre": up_pre, "grad_out": grad_out, "codes": codes, "scales": scales}


def decode(codes, scales):
    factor = jnp.exp2(scales.astype(jnp.float32) - 127.0).astype(jnp.bfloat16)
    blocks = codes.reshape(FF // 32, 32, D) * factor[:, None, :]
    return blocks.reshape(FF, D)


def reference(gate_pre, up_pre, grad_out, codes, scales):
    weight = decode(codes, scales)
    gate_value = gate_pre.astype(jnp.float32)
    up_value = up_pre.astype(jnp.float32)
    sigmoid_gate = jax.nn.sigmoid(gate_value)
    hidden = (gate_value * sigmoid_gate * up_value).astype(jnp.bfloat16)
    width = FF // N_TENSOR

    def add_block(index, total):
        start = (index * width).astype(jnp.int32)
        hidden_block = lax.dynamic_slice_in_dim(hidden, start, width, 1)
        weight_block = lax.dynamic_slice_in_dim(weight, start, width, 0)
        partial_sum = jnp.dot(hidden_block, weight_block, preferred_element_type=jnp.float32).astype(jnp.bfloat16)
        return total + lax.optimization_barrier(partial_sum).astype(jnp.float32)

    out = lax.fori_loop(0, N_TENSOR, add_block, jnp.zeros((TOKENS, D), jnp.float32)).astype(jnp.bfloat16)
    grad_hidden = jnp.dot(grad_out, weight.T, preferred_element_type=jnp.float32)
    grad_gate = (grad_hidden * up_value * sigmoid_gate * (1.0 + gate_value * (1.0 - sigmoid_gate))).astype(jnp.bfloat16)
    grad_up = (grad_hidden * gate_value * sigmoid_gate).astype(jnp.bfloat16)

    def add_replica(index, total):
        start = (index * TOK_DEV).astype(jnp.int32)
        hidden_rows = lax.dynamic_slice_in_dim(hidden, start, TOK_DEV, 0)
        grad_rows = lax.dynamic_slice_in_dim(grad_out, start, TOK_DEV, 0)
        partial_sum = jnp.dot(hidden_rows.T, grad_rows, preferred_element_type=jnp.float32).astype(jnp.bfloat16)
        return total + lax.optimization_barrier(partial_sum).astype(jnp.float32)

    grad_weight = lax.fori_loop(0, N_DP, add_replica, jnp.zeros((FF, D), jnp.float32)).astype(jnp.bfloat16)
    return (out, grad_gate, grad_up, grad_weight)
```

```python
import functools

import jax
import jax.numpy as jnp
from jax import lax
from jax.experimental import pallas as pl
from jax.experimental.pallas import tpu as pltpu
from jax.sharding import PartitionSpec as P


def decode(codes, scales):
    factor = jnp.exp2(scales.astype(jnp.float32) - 127.0).astype(jnp.bfloat16)
    blocks = codes.reshape(scales.shape[0], 32, codes.shape[1]) * factor[:, None, :]
    return blocks.reshape(codes.shape)


def exchange(value, bits, n):
    return lax.ppermute(value, "dp", [(d, d ^ bits) for d in range(n)])


def gather_hidden(halves, n):
    blocks = {0: halves}
    for j in sorted(range(2, n, 2), key=lambda j: bin(j).count("1")):
        low, high = j & -j, 1 << (j.bit_length() - 1)
        blocks[j] = (
            exchange(blocks[j ^ low][0], low, n),
            exchange(blocks[j ^ high][1], high, n),
        )
    for j in range(1, n, 2):
        blocks[j] = tuple(exchange(half, 1, n) for half in blocks[j - 1])
    return blocks


def hidden_kernel(cut, gate_ref, up_ref, whole_ref, low_ref, high_ref):
    gate_value = gate_ref[...].astype(jnp.float32)
    value = gate_value * jax.nn.sigmoid(gate_value) * up_ref[...].astype(jnp.float32)
    value = value.astype(jnp.bfloat16)
    whole_ref[...] = value
    low_ref[...] = value[:, :cut]
    high_ref[...] = value[:, cut:]


def gated(gate_pre, up_pre, cut):
    rows, ff = gate_pre.shape
    step = 64
    widths = (ff, cut, ff - cut)
    spec = [pl.BlockSpec((step, width), lambda i: (i, 0)) for width in widths]
    return pl.pallas_call(
        functools.partial(hidden_kernel, cut),
        grid=(rows // step,),
        in_specs=[spec[0], spec[0]],
        out_specs=spec,
        out_shape=[jax.ShapeDtypeStruct((rows, width), jnp.bfloat16) for width in widths],
        compiler_params=pltpu.CompilerParams(vmem_limit_bytes=24 * 2**20),
        cost_estimate=pl.CostEstimate(
            flops=8 * rows * ff, bytes_accessed=8 * rows * ff, transcendentals=rows * ff
        ),
    )(gate_pre, up_pre)


def make_per_device(n):
    def per_device(gate_pre, up_pre, grad_out, codes, scales):
        me = lax.axis_index("dp")
        cotangent = lax.all_gather(grad_out, "tensor", axis=0, tiled=True)

        ff = gate_pre.shape[1]
        cut = max(256, ff // 512 * 256)
        gate_value = gate_pre.astype(jnp.float32)
        up_value = up_pre.astype(jnp.float32)
        sigmoid_gate = jax.nn.sigmoid(gate_value)
        hidden, low, high = gated(gate_pre, up_pre, cut)
        blocks = gather_hidden((low, high), n)

        weight = decode(codes, scales)
        out = lax.psum_scatter(
            jnp.dot(hidden, weight, preferred_element_type=jnp.float32).astype(jnp.bfloat16),
            "tensor",
            scatter_dimension=0,
            tiled=True,
        )

        width = cotangent.shape[1] // n
        columns = {}
        for j in range(n):
            part = lax.dynamic_slice_in_dim(cotangent, (me ^ j) * width, width, 1)
            columns[j] = exchange(part, j, n) if j else part

        grad_hidden = lax.dot_general(
            cotangent, weight, (((1,), (1,)), ((), ())), preferred_element_type=jnp.float32
        )
        grad_gate = (
            grad_hidden * up_value * sigmoid_gate * (1.0 + gate_value * (1.0 - sigmoid_gate))
        ).astype(jnp.bfloat16)
        grad_up = (grad_hidden * gate_value * sigmoid_gate).astype(jnp.bfloat16)

        order = sorted(range(n), key=lambda j: (bin(j >> 1).count("1"), j))
        rows = []
        for half in (0, 1):
            total = None
            for j in order:
                term = lax.dot_general(
                    blocks[j][half],
                    columns[j],
                    (((0,), (0,)), ((), ())),
                    preferred_element_type=jnp.float32,
                )
                total = term if total is None else total + term
            rows.append(total.astype(jnp.bfloat16))
        grad_weight = jnp.concatenate(rows, axis=0)
        return (out, grad_gate, grad_up, grad_weight)

    return per_device


def solution(mesh):
    in_specs = (
        P("dp", "tensor"),
        P("dp", "tensor"),
        P(("dp", "tensor"), None),
        P("tensor", None),
        P("tensor", None),
    )
    out_specs = (P(("dp", "tensor"), None), P("dp", "tensor"), P("dp", "tensor"), P("tensor", "dp"))
    return jax.shard_map(
        make_per_device(mesh.shape["dp"]),
        mesh=mesh,
        in_specs=in_specs,
        out_specs=out_specs,
        check_vma=False,
    )
```

```python
import functools

import jax
import jax.numpy as jnp
from jax import lax
from jax.experimental import pallas as pl
from jax.experimental.pallas import tpu as pltpu
from jax.sharding import PartitionSpec as P


def decoded(codes, factor):
    rows, columns = codes.shape
    blocks = codes.reshape(rows // 32, 32, columns) * factor.astype(jnp.bfloat16)[:, None, :]
    return blocks.reshape(rows, columns)


def tile_of(extent, largest):
    tile = largest
    while extent % tile:
        tile //= 2
    return tile


def forward_kernel(hidden_ref, codes_ref, factor_ref, out_ref):
    weight = decoded(codes_ref[...], factor_ref[...])
    out_ref[...] = jnp.dot(
        hidden_ref[...], weight, preferred_element_type=jnp.float32
    ).astype(jnp.bfloat16)


def forward(hidden, codes, factor):
    rows, ff = hidden.shape
    width = codes.shape[1]
    tile = tile_of(width, 512)
    return pl.pallas_call(
        forward_kernel,
        grid=(width // tile,),
        in_specs=[
            pl.BlockSpec((rows, ff), lambda i: (0, 0)),
            pl.BlockSpec((ff, tile), lambda i: (0, i)),
            pl.BlockSpec((factor.shape[0], tile), lambda i: (0, i)),
        ],
        out_specs=pl.BlockSpec((rows, tile), lambda i: (0, i)),
        out_shape=jax.ShapeDtypeStruct((rows, width), jnp.bfloat16),
        compiler_params=pltpu.CompilerParams(vmem_limit_bytes=40 * 2**20),
        cost_estimate=pl.CostEstimate(
            flops=2 * rows * ff * width,
            bytes_accessed=2 * (rows * ff + ff * width + rows * width),
            transcendentals=0,
        ),
    )(hidden, codes, factor)


def backward_kernel(cot_ref, codes_ref, factor_ref, gate_ref, up_ref, grad_gate_ref, grad_up_ref):
    weight = decoded(codes_ref[...], factor_ref[0])
    grad_hidden = lax.dot_general(
        cot_ref[...], weight, (((1,), (1,)), ((), ())), preferred_element_type=jnp.float32
    )
    gate = gate_ref[...].astype(jnp.float32)
    up = up_ref[...].astype(jnp.float32)
    sigmoid = jax.nn.sigmoid(gate)
    scaled = grad_hidden * sigmoid
    grad_gate_ref[...] = (scaled * up * (1.0 + gate * (1.0 - sigmoid))).astype(jnp.bfloat16)
    grad_up_ref[...] = (scaled * gate).astype(jnp.bfloat16)


def backward(cotangent, codes, factor, gate_pre, up_pre):
    rows, width = cotangent.shape
    ff = codes.shape[0]
    tile = tile_of(ff, 512)
    factor = factor.reshape(ff // tile, tile // 32, width)
    column = pl.BlockSpec((rows, tile), lambda i: (0, i))
    return pl.pallas_call(
        backward_kernel,
        grid=(ff // tile,),
        in_specs=[
            pl.BlockSpec((rows, width), lambda i: (0, 0)),
            pl.BlockSpec((tile, width), lambda i: (i, 0)),
            pl.BlockSpec((1, tile // 32, width), lambda i: (i, 0, 0)),
            column,
            column,
        ],
        out_specs=[column, column],
        out_shape=[jax.ShapeDtypeStruct((rows, ff), jnp.bfloat16)] * 2,
        compiler_params=pltpu.CompilerParams(vmem_limit_bytes=40 * 2**20),
        cost_estimate=pl.CostEstimate(
            flops=2 * rows * ff * width,
            bytes_accessed=2 * (4 * rows * ff + ff * width + rows * width),
            transcendentals=rows * ff,
        ),
    )(cotangent, codes, factor, gate_pre, up_pre)


def turn_kernel(cot_ref, *rest):
    rest[-1][...] = cot_ref[...].astype(jnp.float32).T.astype(jnp.bfloat16)


def turn(cotangent, after):
    rows, width = cotangent.shape
    tile = tile_of(width, 512)
    return pl.pallas_call(
        turn_kernel,
        grid=(width // tile,),
        in_specs=[pl.BlockSpec((rows, tile), lambda i: (0, i))]
        + [pl.BlockSpec(memory_space=pl.ANY)] * len(after),
        out_specs=pl.BlockSpec((tile, rows), lambda i: (i, 0)),
        out_shape=jax.ShapeDtypeStruct((width, rows), jnp.bfloat16),
        compiler_params=pltpu.CompilerParams(vmem_limit_bytes=24 * 2**20),
        cost_estimate=pl.CostEstimate(
            flops=0, bytes_accessed=4 * rows * width, transcendentals=0
        ),
    )(cotangent, *after)


def product_kernel(n, *refs):
    hidden, columns, out_ref = refs[:n], refs[n : 2 * n], refs[2 * n]
    total = None
    for h_ref, c_ref in zip(hidden, columns):
        term = jnp.dot(c_ref[...], h_ref[...], preferred_element_type=jnp.float32)
        total = term if total is None else total + term
    out_ref[...] = total.T.astype(jnp.bfloat16)


def products(hidden, columns):
    n = len(hidden)
    tokens, ff = hidden[0].shape
    width = columns[0].shape[0]
    tile = tile_of(ff, 256)
    return pl.pallas_call(
        functools.partial(product_kernel, n),
        grid=(ff // tile,),
        in_specs=[pl.BlockSpec((tokens, tile), lambda i: (0, i))] * n
        + [pl.BlockSpec((width, tokens), lambda i: (0, 0))] * n,
        out_specs=pl.BlockSpec((tile, width), lambda i: (i, 0)),
        out_shape=jax.ShapeDtypeStruct((ff, width), jnp.bfloat16),
        compiler_params=pltpu.CompilerParams(vmem_limit_bytes=40 * 2**20),
        cost_estimate=pl.CostEstimate(
            flops=2 * n * tokens * ff * width,
            bytes_accessed=2 * (n * tokens * (ff + width) + ff * width),
            transcendentals=0,
        ),
    )(*hidden, *columns)


def exchange(value, bits, n):
    return lax.ppermute(value, "dp", [(d, d ^ bits) for d in range(n)])


def gather_hidden(halves, n):
    blocks = {0: halves}
    for j in sorted(range(2, n, 2), key=lambda j: bin(j).count("1")):
        low, high = j & -j, 1 << (j.bit_length() - 1)
        blocks[j] = (
            exchange(blocks[j ^ low][0], low, n),
            exchange(blocks[j ^ high][1], high, n),
        )
    for j in range(1, n, 2):
        blocks[j] = tuple(exchange(half, 1, n) for half in blocks[j - 1])
    return blocks


def hidden_kernel(cut, gate_ref, up_ref, whole_ref, low_ref, high_ref):
    gate_value = gate_ref[...].astype(jnp.float32)
    value = gate_value * jax.nn.sigmoid(gate_value) * up_ref[...].astype(jnp.float32)
    value = value.astype(jnp.bfloat16)
    whole_ref[...] = value
    low_ref[...] = value[:, :cut]
    high_ref[...] = value[:, cut:]


def gated(gate_pre, up_pre, cut):
    rows, ff = gate_pre.shape
    step = 64
    widths = (ff, cut, ff - cut)
    spec = [pl.BlockSpec((step, width), lambda i: (i, 0)) for width in widths]
    return pl.pallas_call(
        functools.partial(hidden_kernel, cut),
        grid=(rows // step,),
        in_specs=[spec[0], spec[0]],
        out_specs=spec,
        out_shape=[jax.ShapeDtypeStruct((rows, width), jnp.bfloat16) for width in widths],
        compiler_params=pltpu.CompilerParams(vmem_limit_bytes=24 * 2**20),
        cost_estimate=pl.CostEstimate(
            flops=8 * rows * ff, bytes_accessed=8 * rows * ff, transcendentals=rows * ff
        ),
    )(gate_pre, up_pre)


def make_per_device(n):
    def per_device(gate_pre, up_pre, grad_out, codes, scales):
        me = lax.axis_index("dp")
        cotangent = lax.all_gather(grad_out, "tensor", axis=0, tiled=True)

        ff = gate_pre.shape[1]
        cut = max(256, ff // 512 * 256)
        gate_value = gate_pre.astype(jnp.float32)
        up_value = up_pre.astype(jnp.float32)
        sigmoid_gate = jax.nn.sigmoid(gate_value)
        hidden, low, high = gated(gate_pre, up_pre, cut)
        blocks = gather_hidden((low, high), n)

        first = [half for j in range(2, n, 2) if j & (j - 1) == 0 for half in blocks[j]]
        factor = jnp.exp2(scales.astype(jnp.float32) - 127.0)
        partial_out = forward(hidden, codes, factor)
        out = lax.psum_scatter(partial_out, "tensor", scatter_dimension=0, tiled=True)

        width = cotangent.shape[1] // n
        turned = turn(cotangent, [partial_out, *first])
        pairs = []
        for j in range(0, n, 2):
            start = ((me ^ j) // 2) * (2 * width)
            pair = lax.dynamic_slice_in_dim(turned, start, 2 * width, 0)
            pairs.append(exchange(pair, j, n) if j else pair)
        core = me % 2
        kept = [lax.dynamic_slice_in_dim(pair, core * width, width, 0) for pair in pairs]
        given = [lax.dynamic_slice_in_dim(pair, (1 - core) * width, width, 0) for pair in pairs]
        taken = exchange(jnp.concatenate(given, axis=0), 1, n)
        columns = {}
        for m in range(n // 2):
            columns[2 * m] = kept[m]
            columns[2 * m + 1] = taken[m * width : (m + 1) * width]

        grad_gate, grad_up = backward(cotangent, codes, factor, gate_pre, up_pre)

        grad_weight = jnp.concatenate(
            [
                products([blocks[j][half] for j in range(n)], [columns[j] for j in range(n)])
                for half in (0, 1)
            ],
            axis=0,
        )
        return (out, grad_gate, grad_up, grad_weight)

    return per_device


def solution(mesh):
    in_specs = (
        P("dp", "tensor"),
        P("dp", "tensor"),
        P(("dp", "tensor"), None),
        P("tensor", None),
        P("tensor", None),
    )
    out_specs = (P(("dp", "tensor"), None), P("dp", "tensor"), P("dp", "tensor"), P("tensor", "dp"))
    return jax.shard_map(
        make_per_device(mesh.shape["dp"]),
        mesh=mesh,
        in_specs=in_specs,
        out_specs=out_specs,
        check_vma=False,
    )
```

```python
import functools

import jax
import jax.numpy as jnp
from jax import lax
from jax.experimental import pallas as pl
from jax.experimental.pallas import tpu as pltpu
from jax.sharding import PartitionSpec as P


def decoded(codes, factor):
    rows, columns = codes.shape
    blocks = codes.reshape(rows // 32, 32, columns) * factor.astype(jnp.bfloat16)[:, None, :]
    return blocks.reshape(rows, columns)


def tile_of(extent, largest):
    tile = largest
    while extent % tile:
        tile //= 2
    return tile


def forward_kernel(hidden_ref, codes_ref, factor_ref, out_ref):
    weight = decoded(codes_ref[...], factor_ref[...])
    out_ref[...] = jnp.dot(
        hidden_ref[...], weight, preferred_element_type=jnp.float32
    ).astype(jnp.bfloat16)


def forward(hidden, codes, factor):
    rows, ff = hidden.shape
    width = codes.shape[1]
    tile = tile_of(width, 512)
    return pl.pallas_call(
        forward_kernel,
        grid=(width // tile,),
        in_specs=[
            pl.BlockSpec((rows, ff), lambda i: (0, 0)),
            pl.BlockSpec((ff, tile), lambda i: (0, i)),
            pl.BlockSpec((factor.shape[0], tile), lambda i: (0, i)),
        ],
        out_specs=pl.BlockSpec((rows, tile), lambda i: (0, i)),
        out_shape=jax.ShapeDtypeStruct((rows, width), jnp.bfloat16),
        compiler_params=pltpu.CompilerParams(vmem_limit_bytes=40 * 2**20),
        cost_estimate=pl.CostEstimate(
            flops=2 * rows * ff * width,
            bytes_accessed=2 * (rows * ff + ff * width + rows * width),
            transcendentals=0,
        ),
    )(hidden, codes, factor)


def backward_kernel(cot_ref, codes_ref, factor_ref, gate_ref, up_ref, grad_gate_ref, grad_up_ref):
    weight = decoded(codes_ref[...], factor_ref[0])
    grad_hidden = lax.dot_general(
        cot_ref[...], weight, (((1,), (1,)), ((), ())), preferred_element_type=jnp.float32
    )
    gate = gate_ref[...].astype(jnp.float32)
    up = up_ref[...].astype(jnp.float32)
    sigmoid = jax.nn.sigmoid(gate)
    scaled = grad_hidden * sigmoid
    grad_gate_ref[...] = (scaled * up * (1.0 + gate * (1.0 - sigmoid))).astype(jnp.bfloat16)
    grad_up_ref[...] = (scaled * gate).astype(jnp.bfloat16)


def backward(cotangent, codes, factor, gate_pre, up_pre):
    rows, width = cotangent.shape
    ff = codes.shape[0]
    tile = tile_of(ff, 512)
    factor = factor.reshape(ff // tile, tile // 32, width)
    column = pl.BlockSpec((rows, tile), lambda i: (0, i))
    return pl.pallas_call(
        backward_kernel,
        grid=(ff // tile,),
        in_specs=[
            pl.BlockSpec((rows, width), lambda i: (0, 0)),
            pl.BlockSpec((tile, width), lambda i: (i, 0)),
            pl.BlockSpec((1, tile // 32, width), lambda i: (i, 0, 0)),
            column,
            column,
        ],
        out_specs=[column, column],
        out_shape=[jax.ShapeDtypeStruct((rows, ff), jnp.bfloat16)] * 2,
        compiler_params=pltpu.CompilerParams(vmem_limit_bytes=40 * 2**20),
        cost_estimate=pl.CostEstimate(
            flops=2 * rows * ff * width,
            bytes_accessed=2 * (4 * rows * ff + ff * width + rows * width),
            transcendentals=rows * ff,
        ),
    )(cotangent, codes, factor, gate_pre, up_pre)


def turn_kernel(cot_ref, *rest):
    rest[-1][...] = cot_ref[...].astype(jnp.float32).T.astype(jnp.bfloat16)


def turn(cotangent, after):
    rows, width = cotangent.shape
    tile = tile_of(width, 512)
    return pl.pallas_call(
        turn_kernel,
        grid=(width // tile,),
        in_specs=[pl.BlockSpec((rows, tile), lambda i: (0, i))]
        + [pl.BlockSpec(memory_space=pl.ANY)] * len(after),
        out_specs=pl.BlockSpec((tile, rows), lambda i: (i, 0)),
        out_shape=jax.ShapeDtypeStruct((width, rows), jnp.bfloat16),
        compiler_params=pltpu.CompilerParams(vmem_limit_bytes=24 * 2**20),
        cost_estimate=pl.CostEstimate(
            flops=0, bytes_accessed=4 * rows * width, transcendentals=0
        ),
    )(cotangent, *after)


def pack_kernel(n, *refs):
    rows = refs[0].shape[0]
    for j in range(n):
        refs[-1][j * rows : (j + 1) * rows, :] = refs[j][...]


def pack(parts, after):
    n, (rows, width) = len(parts), parts[0].shape
    return pl.pallas_call(
        functools.partial(pack_kernel, n),
        in_specs=[pl.BlockSpec(memory_space=pltpu.VMEM)] * n
        + [pl.BlockSpec(memory_space=pl.ANY)] * len(after),
        out_specs=pl.BlockSpec(memory_space=pltpu.VMEM),
        out_shape=jax.ShapeDtypeStruct((n * rows, width), parts[0].dtype),
        compiler_params=pltpu.CompilerParams(vmem_limit_bytes=24 * 2**20),
        cost_estimate=pl.CostEstimate(
            flops=0, bytes_accessed=4 * n * rows * width, transcendentals=0
        ),
    )(*parts, *after)


def product_kernel(n, *refs):
    hidden, columns, out_ref = refs[:n], refs[n : 2 * n], refs[2 * n]
    total = None
    for h_ref, c_ref in zip(hidden, columns):
        term = jnp.dot(c_ref[...], h_ref[...], preferred_element_type=jnp.float32)
        total = term if total is None else total + term
    out_ref[...] = total.T.astype(jnp.bfloat16)


def products(hidden, columns):
    n = len(hidden)
    tokens, ff = hidden[0].shape
    width = columns[0].shape[0]
    tile = tile_of(ff, 256)
    return pl.pallas_call(
        functools.partial(product_kernel, n),
        grid=(ff // tile,),
        in_specs=[pl.BlockSpec((tokens, tile), lambda i: (0, i))] * n
        + [pl.BlockSpec((width, tokens), lambda i: (0, 0))] * n,
        out_specs=pl.BlockSpec((tile, width), lambda i: (i, 0)),
        out_shape=jax.ShapeDtypeStruct((ff, width), jnp.bfloat16),
        compiler_params=pltpu.CompilerParams(vmem_limit_bytes=40 * 2**20),
        cost_estimate=pl.CostEstimate(
            flops=2 * n * tokens * ff * width,
            bytes_accessed=2 * (n * tokens * (ff + width) + ff * width),
            transcendentals=0,
        ),
    )(*hidden, *columns)


def exchange(value, bits, n):
    return lax.ppermute(value, "dp", [(d, d ^ bits) for d in range(n)])


def gather_hidden(halves, n):
    blocks = {0: halves}
    for j in sorted(range(2, n, 2), key=lambda j: bin(j).count("1")):
        low, high = j & -j, 1 << (j.bit_length() - 1)
        blocks[j] = (
            exchange(blocks[j ^ low][0], low, n),
            exchange(blocks[j ^ high][1], high, n),
        )
    for j in range(1, n, 2):
        blocks[j] = tuple(exchange(half, 1, n) for half in blocks[j - 1])
    return blocks


def hidden_kernel(cut, gate_ref, up_ref, whole_ref, low_ref, high_ref):
    gate_value = gate_ref[...].astype(jnp.float32)
    value = gate_value * jax.nn.sigmoid(gate_value) * up_ref[...].astype(jnp.float32)
    value = value.astype(jnp.bfloat16)
    whole_ref[...] = value
    low_ref[...] = value[:, :cut]
    high_ref[...] = value[:, cut:]


def gated(gate_pre, up_pre, cut):
    rows, ff = gate_pre.shape
    step = 64
    widths = (ff, cut, ff - cut)
    spec = [pl.BlockSpec((step, width), lambda i: (i, 0)) for width in widths]
    return pl.pallas_call(
        functools.partial(hidden_kernel, cut),
        grid=(rows // step,),
        in_specs=[spec[0], spec[0]],
        out_specs=spec,
        out_shape=[jax.ShapeDtypeStruct((rows, width), jnp.bfloat16) for width in widths],
        compiler_params=pltpu.CompilerParams(vmem_limit_bytes=24 * 2**20),
        cost_estimate=pl.CostEstimate(
            flops=8 * rows * ff, bytes_accessed=8 * rows * ff, transcendentals=rows * ff
        ),
    )(gate_pre, up_pre)


def make_per_device(n):
    def per_device(gate_pre, up_pre, grad_out, codes, scales):
        me = lax.axis_index("dp")
        cotangent = lax.all_gather(grad_out, "tensor", axis=0, tiled=True)

        ff = gate_pre.shape[1]
        cut = max(256, ff // 512 * 256)
        gate_value = gate_pre.astype(jnp.float32)
        up_value = up_pre.astype(jnp.float32)
        sigmoid_gate = jax.nn.sigmoid(gate_value)
        hidden, low, high = gated(gate_pre, up_pre, cut)
        blocks = gather_hidden((low, high), n)

        first = [half for j in range(2, n, 2) if j & (j - 1) == 0 for half in blocks[j]]
        factor = jnp.exp2(scales.astype(jnp.float32) - 127.0)
        partial_out = forward(hidden, codes, factor)
        out = lax.psum_scatter(partial_out, "tensor", scatter_dimension=0, tiled=True)

        width = cotangent.shape[1] // n
        turned = turn(cotangent, [partial_out, *first])
        pairs = []
        for j in range(0, n, 2):
            start = ((me ^ j) // 2) * (2 * width)
            pair = lax.dynamic_slice_in_dim(turned, start, 2 * width, 0)
            pairs.append(exchange(pair, j, n) if j else pair)
        core = me % 2
        kept = [lax.dynamic_slice_in_dim(pair, core * width, width, 0) for pair in pairs]
        given = [lax.dynamic_slice_in_dim(pair, (1 - core) * width, width, 0) for pair in pairs]
        grad_gate, grad_up = backward(cotangent, codes, factor, gate_pre, up_pre)
        second = [half for j in range(2, n, 2) if j & (j - 1) for half in blocks[j]]
        taken = exchange(pack(given, [grad_up, *second]), 1, n)
        columns = {}
        for m in range(n // 2):
            columns[2 * m] = kept[m]
            columns[2 * m + 1] = taken[m * width : (m + 1) * width]

        grad_weight = jnp.concatenate(
            [
                products([blocks[j][half] for j in range(n)], [columns[j] for j in range(n)])
                for half in (0, 1)
            ],
            axis=0,
        )
        return (out, grad_gate, grad_up, grad_weight)

    return per_device


def solution(mesh):
    in_specs = (
        P("dp", "tensor"),
        P("dp", "tensor"),
        P(("dp", "tensor"), None),
        P("tensor", None),
        P("tensor", None),
    )
    out_specs = (P(("dp", "tensor"), None), P("dp", "tensor"), P("dp", "tensor"), P("tensor", "dp"))
    return jax.shard_map(
        make_per_device(mesh.shape["dp"]),
        mesh=mesh,
        in_specs=in_specs,
        out_specs=out_specs,
        check_vma=False,
    )
```

```python
import functools

import jax
import jax.numpy as jnp
from jax import lax
from jax.experimental import pallas as pl
from jax.experimental.pallas import tpu as pltpu
from jax.sharding import PartitionSpec as P


def decoded(codes, factor):
    rows, columns = codes.shape
    blocks = codes.reshape(rows // 32, 32, columns) * factor.astype(jnp.bfloat16)[:, None, :]
    return blocks.reshape(rows, columns)


def tile_of(extent, largest):
    tile = largest
    while extent % tile:
        tile //= 2
    return tile


def forward_kernel(hidden_ref, codes_ref, factor_ref, out_ref):
    weight = decoded(codes_ref[...], factor_ref[...])
    out_ref[...] = jnp.dot(
        hidden_ref[...], weight, preferred_element_type=jnp.float32
    ).astype(jnp.bfloat16)


def forward(hidden, codes, factor):
    rows, ff = hidden.shape
    width = codes.shape[1]
    tile = tile_of(width, 512)
    return pl.pallas_call(
        forward_kernel,
        grid=(width // tile,),
        in_specs=[
            pl.BlockSpec((rows, ff), lambda i: (0, 0)),
            pl.BlockSpec((ff, tile), lambda i: (0, i)),
            pl.BlockSpec((factor.shape[0], tile), lambda i: (0, i)),
        ],
        out_specs=pl.BlockSpec((rows, tile), lambda i: (0, i)),
        out_shape=jax.ShapeDtypeStruct((rows, width), jnp.bfloat16),
        compiler_params=pltpu.CompilerParams(vmem_limit_bytes=40 * 2**20),
        cost_estimate=pl.CostEstimate(
            flops=2 * rows * ff * width,
            bytes_accessed=2 * (rows * ff + ff * width + rows * width),
            transcendentals=0,
        ),
    )(hidden, codes, factor)


def backward_kernel(cot_ref, codes_ref, factor_ref, gate_ref, up_ref, grad_gate_ref, grad_up_ref):
    weight = decoded(codes_ref[...], factor_ref[0])
    grad_hidden = lax.dot_general(
        cot_ref[...], weight, (((1,), (1,)), ((), ())), preferred_element_type=jnp.float32
    )
    gate = gate_ref[...].astype(jnp.float32)
    up = up_ref[...].astype(jnp.float32)
    sigmoid = jax.nn.sigmoid(gate)
    scaled = grad_hidden * sigmoid
    grad_gate_ref[...] = (scaled * up * (1.0 + gate * (1.0 - sigmoid))).astype(jnp.bfloat16)
    grad_up_ref[...] = (scaled * gate).astype(jnp.bfloat16)


def backward(cotangent, codes, factor, gate_pre, up_pre):
    rows, width = cotangent.shape
    ff = codes.shape[0]
    tile = tile_of(ff, 512)
    factor = factor.reshape(ff // tile, tile // 32, width)
    column = pl.BlockSpec((rows, tile), lambda i: (0, i))
    return pl.pallas_call(
        backward_kernel,
        grid=(ff // tile,),
        in_specs=[
            pl.BlockSpec((rows, width), lambda i: (0, 0)),
            pl.BlockSpec((tile, width), lambda i: (i, 0)),
            pl.BlockSpec((1, tile // 32, width), lambda i: (i, 0, 0)),
            column,
            column,
        ],
        out_specs=[column, column],
        out_shape=[jax.ShapeDtypeStruct((rows, ff), jnp.bfloat16)] * 2,
        compiler_params=pltpu.CompilerParams(vmem_limit_bytes=40 * 2**20),
        cost_estimate=pl.CostEstimate(
            flops=2 * rows * ff * width,
            bytes_accessed=2 * (4 * rows * ff + ff * width + rows * width),
            transcendentals=rows * ff,
        ),
    )(cotangent, codes, factor, gate_pre, up_pre)


def turn_kernel(cot_ref, *rest):
    rest[-1][...] = cot_ref[...].astype(jnp.float32).T.astype(jnp.bfloat16)


def turn(cotangent, after):
    rows, width = cotangent.shape
    tile = tile_of(width, 512)
    return pl.pallas_call(
        turn_kernel,
        grid=(width // tile,),
        in_specs=[pl.BlockSpec((rows, tile), lambda i: (0, i))]
        + [pl.BlockSpec(memory_space=pl.ANY)] * len(after),
        out_specs=pl.BlockSpec((tile, rows), lambda i: (i, 0)),
        out_shape=jax.ShapeDtypeStruct((width, rows), jnp.bfloat16),
        compiler_params=pltpu.CompilerParams(vmem_limit_bytes=24 * 2**20),
        cost_estimate=pl.CostEstimate(
            flops=0, bytes_accessed=4 * rows * width, transcendentals=0
        ),
    )(cotangent, *after)


def pack_kernel(n, *refs):
    rows = refs[0].shape[0]
    for j in range(n):
        refs[-1][j * rows : (j + 1) * rows, :] = refs[j][...]


def pack(parts, after):
    n, (rows, width) = len(parts), parts[0].shape
    return pl.pallas_call(
        functools.partial(pack_kernel, n),
        in_specs=[pl.BlockSpec(memory_space=pltpu.VMEM)] * n
        + [pl.BlockSpec(memory_space=pl.ANY)] * len(after),
        out_specs=pl.BlockSpec(memory_space=pltpu.VMEM),
        out_shape=jax.ShapeDtypeStruct((n * rows, width), parts[0].dtype),
        compiler_params=pltpu.CompilerParams(vmem_limit_bytes=24 * 2**20),
        cost_estimate=pl.CostEstimate(
            flops=0, bytes_accessed=4 * n * rows * width, transcendentals=0
        ),
    )(*parts, *after)


def product_kernel(n, *refs):
    hidden, columns, out_ref = refs[:n], refs[n : 2 * n], refs[2 * n]
    total = None
    for h_ref, c_ref in zip(hidden, columns):
        term = jnp.dot(c_ref[...], h_ref[...], preferred_element_type=jnp.float32)
        total = term if total is None else total + term
    out_ref[...] = total.T.astype(jnp.bfloat16)


def products(hidden, columns):
    n = len(hidden)
    tokens, ff = hidden[0].shape
    width = columns[0].shape[0]
    tile = tile_of(ff, 256)
    return pl.pallas_call(
        functools.partial(product_kernel, n),
        grid=(ff // tile,),
        in_specs=[pl.BlockSpec((tokens, tile), lambda i: (0, i))] * n
        + [pl.BlockSpec((width, tokens), lambda i: (0, 0))] * n,
        out_specs=pl.BlockSpec((tile, width), lambda i: (i, 0)),
        out_shape=jax.ShapeDtypeStruct((ff, width), jnp.bfloat16),
        compiler_params=pltpu.CompilerParams(vmem_limit_bytes=40 * 2**20),
        cost_estimate=pl.CostEstimate(
            flops=2 * n * tokens * ff * width,
            bytes_accessed=2 * (n * tokens * (ff + width) + ff * width),
            transcendentals=0,
        ),
    )(*hidden, *columns)


def exchange(value, bits, n):
    return lax.ppermute(value, "dp", [(d, d ^ bits) for d in range(n)])


def gather_hidden(halves, n):
    blocks = {0: halves}
    for j in sorted(range(2, n, 2), key=lambda j: bin(j).count("1")):
        low, high = j & -j, 1 << (j.bit_length() - 1)
        blocks[j] = (
            exchange(blocks[j ^ low][0], low, n),
            exchange(blocks[j ^ high][1], high, n),
        )
    for j in range(1, n, 2):
        blocks[j] = tuple(exchange(half, 1, n) for half in blocks[j - 1])
    return blocks


def hidden_kernel(cut, gate_ref, up_ref, whole_ref, low_ref, high_ref):
    gate_value = gate_ref[...].astype(jnp.float32)
    value = gate_value * jax.nn.sigmoid(gate_value) * up_ref[...].astype(jnp.float32)
    value = value.astype(jnp.bfloat16)
    whole_ref[...] = value
    low_ref[...] = value[:, :cut]
    high_ref[...] = value[:, cut:]


def gated(gate_pre, up_pre, cut):
    rows, ff = gate_pre.shape
    step = 64
    widths = (ff, cut, ff - cut)
    spec = [pl.BlockSpec((step, width), lambda i: (i, 0)) for width in widths]
    return pl.pallas_call(
        functools.partial(hidden_kernel, cut),
        grid=(rows // step,),
        in_specs=[spec[0], spec[0]],
        out_specs=spec,
        out_shape=[jax.ShapeDtypeStruct((rows, width), jnp.bfloat16) for width in widths],
        compiler_params=pltpu.CompilerParams(vmem_limit_bytes=24 * 2**20),
        cost_estimate=pl.CostEstimate(
            flops=8 * rows * ff, bytes_accessed=8 * rows * ff, transcendentals=rows * ff
        ),
    )(gate_pre, up_pre)


def make_per_device(n):
    def per_device(gate_pre, up_pre, grad_out, codes, scales):
        me = lax.axis_index("dp")
        cotangent = lax.all_gather(grad_out, "tensor", axis=0, tiled=True)

        ff = gate_pre.shape[1]
        cut = max(256, ff // 512 * 256)
        gate_value = gate_pre.astype(jnp.float32)
        up_value = up_pre.astype(jnp.float32)
        sigmoid_gate = jax.nn.sigmoid(gate_value)
        hidden, low, high = gated(gate_pre, up_pre, cut)
        blocks = gather_hidden((low, high), n)

        first = [half for j in range(2, n, 2) if j & (j - 1) == 0 for half in blocks[j]]
        factor = jnp.exp2(scales.astype(jnp.float32) - 127.0)
        partial_out = forward(hidden, codes, factor)
        out = lax.psum_scatter(partial_out, "tensor", scatter_dimension=0, tiled=True)

        width = cotangent.shape[1] // n
        turned = turn(cotangent, [partial_out, *first])
        pairs = []
        for j in range(0, n, 2):
            start = ((me ^ j) // 2) * (2 * width)
            pair = lax.dynamic_slice_in_dim(turned, start, 2 * width, 0)
            pairs.append(exchange(pair, j, n) if j else pair)
        core = me % 2
        kept = [lax.dynamic_slice_in_dim(pair, core * width, width, 0) for pair in pairs]
        given = [lax.dynamic_slice_in_dim(pair, (1 - core) * width, width, 0) for pair in pairs]
        grad_gate, grad_up = backward(cotangent, codes, factor, gate_pre, up_pre)
        second = [half for j in range(2, n, 2) if j & (j - 1) for half in blocks[j]]
        other = [blocks[j][0] for j in range(1, n, 2) if (j - 1) & (j - 2) == 0 or j == 1]
        taken = exchange(pack(given, [grad_up, *second, *other]), 1, n)
        columns = {}
        for m in range(n // 2):
            columns[2 * m] = kept[m]
            columns[2 * m + 1] = taken[m * width : (m + 1) * width]

        grad_weight = jnp.concatenate(
            [
                products([blocks[j][half] for j in range(n)], [columns[j] for j in range(n)])
                for half in (0, 1)
            ],
            axis=0,
        )
        return (out, grad_gate, grad_up, grad_weight)

    return per_device


def solution(mesh):
    in_specs = (
        P("dp", "tensor"),
        P("dp", "tensor"),
        P(("dp", "tensor"), None),
        P("tensor", None),
        P("tensor", None),
    )
    out_specs = (P(("dp", "tensor"), None), P("dp", "tensor"), P("dp", "tensor"), P("tensor", "dp"))
    return jax.shard_map(
        make_per_device(mesh.shape["dp"]),
        mesh=mesh,
        in_specs=in_specs,
        out_specs=out_specs,
        check_vma=False,
    )
```
